32 devices in a mesh: row: 16 (over z, x, core), col: 2 (over y).
Axes of the slice: x: 2, y: 2, z: 4, core: 2. Of those that a mesh axis runs over, the one named last changes fastest.
Arguments:
- features: bfloat16 [4096, 128], P(('row', 'col')), may hold values from -6 to 6
- adjacency: bfloat16 [16, 2, 12, 128, 128], P('row', 'col'), may hold values from 0 to 1
- tile_pos: int32 [16, 2, 12], P('row', 'col'), may hold values from 0 to 31, as said below
- tile_count: int32 [16, 2], P('row', 'col'), may hold values from 1 to 12, as said below
- w_self: bfloat16 [128, 256], replicated, may hold values from -0.5 to 0.5
- w_neigh: bfloat16 [128, 256], replicated, may hold values from -0.5 to 0.5
- bias: float32 [256], replicated, may hold values from -3 to 3
- upstream: bfloat16 [4096, 256], P(('row', 'col')), may hold values from -6 to 6
Outputs:
- hidden: bfloat16 [4096, 256], P(('row', 'col'))
- grad_features: bfloat16 [4096, 128], P(('row', 'col'))
- grad_self: float32 [128, 256], replicated
- grad_neigh: float32 [128, 256], replicated
- grad_bias: float32 [256], replicated
The draws below stay inside these ranges and needn't reach their ends.
Inputs may be any that keep to these rules, and one draw needn't show every extreme that they name: `tile_pos`: the positions of a cell's slots are distinct. Some cell has all 12 slots filled; only the first tile_count slots of a cell count.
All inputs are finite; a program needn't handle non-finite values.
Results may differ from the reference program's by a relative error of at most 0.0075.
Values may be sent and summed in bfloat16 or wider, within the bound.
A program may use at most 64 MiB of HBM per device.

```python
import jax
import jax.numpy as jnp
from jax import lax

F = 128
H = 256
TILE = 128
ROW_DEV = 128
ROWB = 256
ROWT = 2
COLT = 16
TILES = 12
NODES = 4096
N_ROW = 16
N_COL = 2


def draw_tile_pos(key, part):
    cell_keys = jax.random.split(jax.random.fold_in(key, 11), N_ROW * N_COL)

    def draw_cell(cell_key):
        return jax.random.permutation(cell_key, ROWT * COLT)[:TILES].astype(jnp.int32)
    return jax.vmap(draw_cell)(cell_keys).reshape(N_ROW, N_COL, TILES)


def draw_tile_count(key, part):
    first_key = jax.random.fold_in(key, 23)
    second_key = jax.random.fold_in(key, 29)
    raw_draw = jax.random.randint(first_key, (N_ROW * N_COL,), 0, TILES + 1)
    counts = jnp.maximum(1, raw_draw * raw_draw // TILES)
    busiest = jax.random.randint(second_key, (), 0, N_ROW * N_COL)
    counts = counts.at[busiest].set(TILES)
    return counts.astype(jnp.int32).reshape(N_ROW, N_COL)


def levels(key, shape, cuts, least, largest):
    level = 1.0
    for dim, blocks in cuts:
        steps = jax.random.uniform(jax.random.fold_in(jax.random.fold_in(key, 6), dim), (blocks,), jnp.float32, least / len(cuts), largest / len(cuts))
        level = level * jnp.repeat(jnp.exp(steps), shape[dim] // blocks).reshape((-1,) + (1,) * (len(shape) - 1 - dim))
    return level


def gaussian(stream_key, shape, spread, limit, shards=(), dtype=jnp.bfloat16):
    drawn = jax.random.normal(stream_key, shape, jnp.float32) * spread
    if len(shards) > 0:
        drawn = levels(stream_key, shape, shards, -0.22, 0.18) * drawn
    return jnp.clip(drawn, min=-limit, max=limit).astype(dtype)


def setup_inputs(seed: int = 0) -> dict:
    splits = jax.random.split(jax.random.key(seed), 9)
    features = gaussian(splits[0], (NODES, F), 1.0, 6.0, ((0, 32),))
    adjacency = jnp.clip(1.0 * jax.random.uniform(splits[1], (N_ROW, N_COL, TILES, TILE, TILE), jnp.float32) ** levels(splits[1], (N_ROW, N_COL, TILES, TILE, TILE), ((0, 16), (1, 2)), -0.2, 0.2), 0.0, 1.0).astype(jnp.bfloat16)
    tile_pos = draw_tile_pos(jax.random.fold_in(splits[8], 71), 0)
    tile_count = draw_tile_count(jax.random.fold_in(splits[8], 71), 0)
    w_self = gaussian(splits[4], (F, H), F ** -0.5, 0.5)
    w_neigh = gaussian(splits[5], (F, H), F ** -0.5, 0.5)
    bias = gaussian(splits[6], (H,), 0.5, 3.0, (), jnp.float32)
    upstream = gaussian(splits[7], (NODES, H), 1.0, 6.0, ((0, 32),))
    return dict(features=features, adjacency=adjacency, tile_pos=tile_pos, tile_count=tile_count, w_self=w_self, w_neigh=w_neigh, bias=bias, upstream=upstream)


def forward_cell(adjacency, position, filled, gathered, row_tiles):
    edge_len = adjacency.shape[1]
    col_tiles = gathered.shape[0] // edge_len
    tile_row = position // col_tiles
    tile_col = position % col_tiles
    usable = jnp.arange(position.shape[0]) < filled
    panel_blocks = gathered.reshape(col_tiles, edge_len, gathered.shape[1])[tile_col]
    products = jnp.einsum('tik,tkf->tif', adjacency.astype(jnp.float32), panel_blocks.astype(jnp.float32), precision=lax.Precision.HIGHEST)
    selector = ((tile_row[None, :] == jnp.arange(row_tiles)[:, None]) & usable[None, :]).astype(jnp.float32)
    partial_value = jnp.einsum('st,tif->sif', selector, products, precision=lax.Precision.HIGHEST).reshape(row_tiles * edge_len, -1)
    row_weights = lax.optimization_barrier(jnp.sum(adjacency.astype(jnp.float32), axis=2))
    degree = jnp.dot(selector, row_weights, precision=lax.Precision.HIGHEST).reshape(-1)
    return (partial_value, degree)

def backward_cell(adjacency, position, filled, grad_rows, col_tiles):
    edge_len = adjacency.shape[1]
    row_tiles = grad_rows.shape[0] // edge_len
    tile_row = position // col_tiles
    tile_col = position % col_tiles
    usable = jnp.arange(position.shape[0]) < filled
    row_blocks = grad_rows.reshape(row_tiles, edge_len, grad_rows.shape[1])[tile_row]
    products = jnp.einsum('tik,tif->tkf', adjacency.astype(jnp.float32), row_blocks.astype(jnp.float32), precision=lax.Precision.HIGHEST)
    selector = ((tile_col[None, :] == jnp.arange(col_tiles)[:, None]) & usable[None, :]).astype(jnp.float32)
    return jnp.einsum('st,tkf->skf', selector, products, precision=lax.Precision.HIGHEST).reshape(col_tiles * edge_len, -1)

def reference(features, adjacency, tile_pos, tile_count, w_self, w_neigh, bias, upstream):
    layout = features.reshape(N_ROW, N_COL, ROW_DEV, F)

    def row_work(row_idx):

        def col_work(col_idx):
            gathered = layout[:, col_idx].reshape(N_ROW * ROW_DEV, F)
            return forward_cell(adjacency[row_idx, col_idx], tile_pos[row_idx, col_idx], tile_count[row_idx, col_idx], gathered, ROWT)
        partials, degrees = lax.map(col_work, jnp.arange(N_COL))
        return (lax.optimization_barrier(jnp.sum(partials, axis=0)), lax.optimization_barrier(jnp.sum(degrees, axis=0)))
    summed, degree = lax.map(row_work, jnp.arange(N_ROW))
    summed = summed.reshape(NODES, F)
    inv_root = 1.0 / jnp.sqrt(1.0 + degree.reshape(NODES))
    aggregate = (summed * inv_root[:, None]).astype(jnp.bfloat16)
    preact = jnp.dot(features, w_self, preferred_element_type=jnp.float32) + jnp.dot(aggregate, w_neigh, preferred_element_type=jnp.float32) + bias
    gate_s = jax.nn.sigmoid(preact)
    hidden = (preact * gate_s).astype(jnp.bfloat16)
    grad_pre = (upstream.astype(jnp.float32) * (gate_s + preact * gate_s * (1.0 - gate_s))).astype(jnp.bfloat16)
    factor = 1.0 / jnp.sqrt(jnp.float32(NODES))
    grad_self = jnp.dot(features.T, grad_pre, preferred_element_type=jnp.float32) * factor
    grad_neigh = jnp.dot(aggregate.T, grad_pre, preferred_element_type=jnp.float32) * factor
    grad_bias = lax.optimization_barrier(jnp.sum(grad_pre.astype(jnp.float32), axis=0)) * factor
    grad_agg = (jnp.dot(grad_pre, w_neigh.T, preferred_element_type=jnp.float32) * inv_root[:, None]).astype(jnp.bfloat16)
    grad_blocks = grad_agg.reshape(N_ROW, ROWB, F)

    def col_back(col_idx):

        def row_back(row_idx):
            return backward_cell(adjacency[row_idx, col_idx], tile_pos[row_idx, col_idx], tile_count[row_idx, col_idx], grad_blocks[row_idx], COLT)
        return lax.optimization_barrier(jnp.sum(lax.map(row_back, jnp.arange(N_ROW)), axis=0))
    back_terms = lax.map(col_back, jnp.arange(N_COL))
    back_terms = back_terms.reshape(N_COL, N_ROW, ROW_DEV, F).transpose(1, 0, 2, 3).reshape(NODES, F)
    grad_features = (jnp.dot(grad_pre, w_self.T, preferred_element_type=jnp.float32) + back_terms).astype(jnp.bfloat16)
    return (hidden, grad_features, grad_self, grad_neigh, grad_bias)
```

```python
import functools
import math

import jax
import jax.numpy as jnp
from jax import lax
from jax.experimental import pallas as pl
from jax.experimental.pallas import tpu as pltpu
from jax.sharding import PartitionSpec as P

BF = jnp.bfloat16
F32 = jnp.float32
MESH = pl.DeviceIdType.MESH


def dot(a, b):
    return jnp.dot(a, b, preferred_element_type=F32)


def dot_nt(a, b):
    return lax.dot_general(a, b, (((1,), (1,)), ((), ())), preferred_element_type=F32)


def kernel(
    n_row, n_col, factor,
    feat, adj, pos, cnt, wself, wneigh, bias, up,
    hid_o, gf_o, gs_o, gn_o, gb_o,
    adj_v, dense, gath, f2, up2, w_v, deg, base, inv_row, inv_col, part, agg_v, gpre, pre,
    c_send, c_recv, own, x_send, x_recv, z_send, z_recv,
    g_units, g1_send, g1_recv, g2_send, g2_recv, gfull,
    loc_sem, send_sem, gath_sem, f2_sem, up_sem, deg_sem, part_sem,
    c_sem, x_sem, z_sem, g1_sem, g2_sem, g3_sem, g4_sem,
):
    row = lax.axis_index("row")
    col = lax.axis_index("col")
    depth = n_row // 4
    half = n_row // 2
    core = row % 2
    x = (row // 2) % 2
    z = row // 4
    tile = feat.shape[0]
    slots = adj.shape[2]
    width = feat.shape[1]
    rows = n_col * tile
    units = g_units.shape[0]
    per = units // n_row

    def row_of(dz, dx, dc):
        return (((z + dz) % depth) * 2 + (x + dx) % 2) * 2 + (core + dc) % 2

    def chip(j):
        return row_of(j % depth, j // depth, 0)

    sends = []

    def send(src, dst, sem, to_row, to_col=None):
        copy = pltpu.make_async_remote_copy(
            src_ref=src, dst_ref=dst, send_sem=send_sem.at[len(sends)], recv_sem=sem,
            device_id=(to_row, col if to_col is None else to_col), device_id_type=MESH,
        )
        copy.start()
        sends.append(copy)

    def got(dst, sem):
        pltpu.make_async_remote_copy(
            src_ref=dst, dst_ref=dst, send_sem=send_sem.at[0], recv_sem=sem,
            device_id=(row_of(0, 0, 1), col), device_id_type=MESH,
        ).wait_recv()

    core_peer = row_of(0, 0, 1)
    x_peer = row_of(0, 1, 0)

    barrier = pltpu.get_barrier_semaphore()
    for j in range(1, half):
        pl.semaphore_signal(barrier, inc=1, device_id=(chip(j), col), device_id_type=MESH)
    pl.semaphore_signal(barrier, inc=1, device_id=(core_peer, col), device_id_type=MESH)
    for k in range(1, n_col):
        pl.semaphore_signal(barrier, inc=1, device_id=(row, (col + k) % n_col), device_id_type=MESH)

    own_rows = pl.ds(pl.multiple_of(col * tile, tile), tile)
    locals_ = [
        pltpu.make_async_copy(adj.at[0, 0], adj_v, loc_sem.at[0]),
        pltpu.make_async_copy(feat, gath.at[pl.ds(0, tile)], loc_sem.at[1]),
        pltpu.make_async_copy(feat, f2.at[own_rows], loc_sem.at[2]),
        pltpu.make_async_copy(up, up2.at[own_rows], loc_sem.at[3]),
        pltpu.make_async_copy(wself, w_v.at[0], loc_sem.at[4]),
        pltpu.make_async_copy(wneigh, w_v.at[1], loc_sem.at[5]),
    ]
    for copy in locals_:
        copy.start()
    pl.semaphore_wait(barrier, half - 1 + 1 + n_col - 1)

    def slot(q):
        return gath.at[pl.ds(q * tile, tile)]

    for k in range(1, depth):
        q = depth - k
        send(feat, slot(q), gath_sem.at[q], row_of(k, 0, 0))
    send(feat, slot(depth), gath_sem.at[depth], x_peer)
    send(feat, slot(half), gath_sem.at[half], core_peer)
    for k in range(1, n_col):
        send(feat, f2.at[own_rows], f2_sem.at[n_col - k], row, (col + k) % n_col)
        send(up, up2.at[own_rows], up_sem.at[n_col - k], row, (col + k) % n_col)

    filled = cnt[0, 0]
    places = [jnp.where(t < filled, pos[0, 0, t], -1) for t in range(slots)]
    locals_[0].wait()

    def place(i, carry):
        r = i // n_row
        q = i % n_row
        target = r * n_row + row_of(q % depth, (q % half) // depth, q // half)
        found = jnp.int32(-1)
        for t in range(slots):
            found = jnp.where(places[t] == target, t, found)
        block = adj_v[jnp.maximum(found, 0)]
        keep = jnp.full((tile, tile), found, jnp.int32) >= 0
        block = jnp.where(keep, block.astype(F32), 0.0).astype(BF)
        dense[pl.ds(pl.multiple_of(r * tile, tile), tile), pl.ds(pl.multiple_of(q * tile, tile), tile)] = block
        return carry

    lax.fori_loop(0, n_col * n_row, place, 0)

    for k in range(1, depth):
        q = depth - k
        got(slot(q), gath_sem.at[q])
        send(slot(q), slot(depth + q), gath_sem.at[depth + q], x_peer)
        send(slot(q), slot(half + q), gath_sem.at[half + q], core_peer)

    ones = jnp.ones((16, dense.shape[1]), BF)
    deg[col] = dot_nt(ones, dense[...])[0:8]
    for k in range(1, n_col):
        send(deg.at[col], deg.at[col], deg_sem.at[n_col - k], row, (col + k) % n_col)

    for q in [depth] + [2 * depth - k for k in range(1, depth)]:
        got(slot(q), gath_sem.at[q])
        send(slot(q), slot(half + q), gath_sem.at[half + q], core_peer)

    locals_[1].wait()
    partial_value = dot(dense[:, : half * tile], gath[: half * tile])

    for copy in locals_[2:]:
        copy.wait()
    for k in range(1, n_col):
        sender = (col + k) % n_col
        sender_rows = pl.ds(pl.multiple_of(sender * tile, tile), tile)
        got(f2.at[sender_rows], f2_sem.at[k])
        got(up2.at[sender_rows], up_sem.at[k])
        got(deg.at[sender], deg_sem.at[k])
    base[...] = dot(f2[...], w_v[0]) + bias[...].reshape(1, -1)
    total = deg[0]
    for k in range(1, n_col):
        total = total + deg[k]
    inv_row[...] = 1.0 / jnp.sqrt(1.0 + total)
    for r in range(n_col):
        line = inv_row[0:1, r * tile : (r + 1) * tile]
        inv_col[r * tile : (r + 1) * tile] = jnp.broadcast_to(line, (tile, tile)).T

    for q in range(half, n_row):
        got(slot(q), gath_sem.at[q])
    partial_value += dot(dense[:, half * tile :], gath[half * tile :])
    part[col] = partial_value.astype(BF)
    for k in range(1, n_col):
        send(part.at[col], part.at[col], part_sem.at[n_col - k], row, (col + k) % n_col)
    for k in range(1, n_col):
        got(part.at[(col + k) % n_col], part_sem.at[k])

    summed = part[0].astype(F32)
    for k in range(1, n_col):
        summed = summed + part[k].astype(F32)
    agg_v[...] = (summed * inv_col[...]).astype(BF)
    pre[...] = base[...] + dot(agg_v[...], w_v[1])
    preact = pre[...]
    gate = jax.nn.sigmoid(preact)
    gpre[...] = (up2[...].astype(F32) * (gate + preact * gate * (1.0 - gate))).astype(BF)
    grad_agg = (dot_nt(w_v[1], gpre[...]) * inv_row[0:1]).astype(BF)

    order = list(range(depth, half)) + list(range(depth))
    for j in order[::2]:
        both = dot(grad_agg, dense[:, (half + j) * tile : (half + j + 2) * tile]).astype(BF)
        for i in (0, 1):
            c_send[j + i] = both[:, i * tile : (i + 1) * tile]
            send(c_send.at[j + i], c_recv.at[j + i], c_sem.at[j + i], core_peer)

    gp = gpre[...]
    upper = dot(f2[...].T, gp)
    lower = dot(agg_v[...].T, gp)
    lanes = gp.shape[1] // 128
    for u in range(units):
        r0, l0 = (u // lanes) * 16, (u % lanes) * 128
        src = upper if r0 < width else lower
        g_units[u] = src[r0 % width : r0 % width + 16, l0 : l0 + 128]
    colsum = dot(jnp.ones((8, gp.shape[0]), BF), gp)
    bias_unit = jnp.concatenate([colsum[:, i * 128 : (i + 1) * 128] for i in range(lanes)], axis=0).astype(BF)
    for j in range(half):
        target = row_of(j % depth, j // depth, 1)
        g1_send[j * per : (j + 1) * per] = g_units[pl.ds(target * per, per)].astype(BF)
    g1_send[half * per] = bias_unit
    send(g1_send, g1_recv, g1_sem.at[0], core_peer)

    for j in order[::2]:
        both = dot(grad_agg, dense[:, j * tile : (j + 2) * tile])
        for i in (0, 1):
            own[j + i] = both[:, i * tile : (i + 1) * tile]

    for dz in list(range(1, depth)) + [0]:
        j = depth + dz
        got(c_recv.at[j], c_sem.at[j])
        x_send[dz] = (own[j] + c_recv[j].astype(F32)).astype(BF)
        send(x_send.at[dz], x_recv.at[dz], x_sem.at[dz], x_peer)

    got(g1_recv, g1_sem.at[0])
    for j in list(range(1, half)) + [0]:
        target = chip(j)
        g2_send[j, 0:per] = (
            g_units[pl.ds(target * per, per)] + g1_recv[j * per : (j + 1) * per].astype(F32)
        ).astype(BF)
        g2_send[j, per] = (bias_unit.astype(F32) + g1_recv[half * per].astype(F32)).astype(BF)
        if j:
            back = (j // depth) * depth + (depth - j % depth) % depth
            send(g2_send.at[j], g2_recv.at[back], g2_sem.at[back], target)
        else:
            g2_recv[0] = g2_send[0]

    for dz in list(range(1, depth)) + [0]:
        got(c_recv.at[dz], c_sem.at[dz])
        got(x_recv.at[dz], x_sem.at[dz])
        value = own[dz] + c_recv[dz].astype(F32) + x_recv[dz].astype(F32)
        if dz:
            z_send[dz - 1] = value.astype(BF)
            send(z_send.at[dz - 1], z_recv.at[dz - 1], z_sem.at[dz - 1], row_of(dz, 0, 0))
        else:
            own[0] = value

    for j in range(1, half):
        got(g2_recv.at[j], g2_sem.at[j])
    piece = jnp.zeros(g2_recv.shape[1:], F32)
    for a in range(half):
        rel = ((a % 2 + 2 - x) % 2) * depth + (a // 2 + depth - z) % depth
        piece = piece + g2_recv[rel].astype(F32)
    piece = piece * factor
    gfull[row] = piece[0:per].astype(BF)
    for j in range(1, half):
        back = (j // depth) * depth + (depth - j % depth) % depth
        send(gfull.at[row], gfull.at[row], g3_sem.at[back], chip(j))
    send(gfull.at[row], gfull.at[row], g4_sem.at[0], core_peer)
    sums = piece[per]
    gb_o[...] = jnp.concatenate([sums[i * 8 : i * 8 + 1] for i in range(lanes)], axis=1).reshape(-1)

    preact = pre[own_rows]
    hid_o[...] = (preact * jax.nn.sigmoid(preact)).astype(BF)
    value = own[0]
    for dz in range(1, depth):
        got(z_recv.at[dz - 1], z_sem.at[dz - 1])
        value = value + z_recv[dz - 1].astype(F32)
    gf_o[...] = (dot_nt(gpre[own_rows], w_v[0]) + value.T).astype(BF)

    for j in range(1, half):
        d = chip(j)
        got(gfull.at[d], g3_sem.at[j])
        send(gfull.at[d], gfull.at[d], g4_sem.at[j], core_peer)
    for j in range(half):
        got(gfull.at[row_of(j % depth, j // depth, 1)], g4_sem.at[j])
    for u in range(units):
        r0, l0 = (u // lanes) * 16, (u % lanes) * 128
        out = gs_o if r0 < width else gn_o
        r0 = r0 % width
        out[r0 : r0 + 16, l0 : l0 + 128] = gfull[u // per, u % per].astype(F32)

    for copy in sends:
        copy.wait_send()


def body(features, adjacency, tile_pos, tile_count, w_self, w_neigh, bias, upstream):
    n_row = lax.axis_size("row")
    n_col = lax.axis_size("col")
    tile, width = features.shape
    hidden = upstream.shape[1]
    slots = adjacency.shape[2]
    rows = n_col * tile
    depth, half = n_row // 4, n_row // 2
    units = (2 * width // 16) * (hidden // 128)
    per = units // n_row
    factor = 1.0 / math.sqrt(tile * n_row * n_col)
    sem = pltpu.SemaphoreType.DMA
    n_sends = (
        (depth - 1) + 2 + 2 * (n_col - 1) + 2 * (depth - 1) + (n_col - 1) + depth + (n_col - 1)
        + half + 1 + depth + (half - 1) + (depth - 1) + (half - 1) + half
    )
    any_ = pl.BlockSpec(memory_space=pl.ANY)
    vmem = pl.BlockSpec(memory_space=pltpu.VMEM)
    smem = pl.BlockSpec(memory_space=pltpu.SMEM)
    scratch = [
        pltpu.VMEM((slots, tile, tile), BF),
        pltpu.VMEM((rows, n_row * tile), BF),
        pltpu.VMEM((n_row * tile, width), BF),
        pltpu.VMEM((rows, width), BF),
        pltpu.VMEM((rows, hidden), BF),
        pltpu.VMEM((2, width, hidden), BF),
        pltpu.VMEM((n_col, 8, rows), F32),
        pltpu.VMEM((rows, hidden), F32),
        pltpu.VMEM((8, rows), F32),
        pltpu.VMEM((rows, width), F32),
        pltpu.VMEM((n_col, rows, width), BF),
        pltpu.VMEM((rows, width), BF),
        pltpu.VMEM((rows, hidden), BF),
        pltpu.VMEM((rows, hidden), F32),
        pltpu.VMEM((half, width, tile), BF),
        pltpu.VMEM((half, width, tile), BF),
        pltpu.VMEM((half, width, tile), F32),
        pltpu.VMEM((depth, width, tile), BF),
        pltpu.VMEM((depth, width, tile), BF),
        pltpu.VMEM((depth - 1, width, tile), BF),
        pltpu.VMEM((depth - 1, width, tile), BF),
        pltpu.VMEM((units, 16, 128), F32),
        pltpu.VMEM((half * per + 1, 16, 128), BF),
        pltpu.VMEM((half * per + 1, 16, 128), BF),
        pltpu.VMEM((half, per + 1, 16, 128), BF),
        pltpu.VMEM((half, per + 1, 16, 128), BF),
        pltpu.VMEM((n_row, per, 16, 128), BF),
        sem((6,)), sem((n_sends,)), sem((n_row,)), sem((n_col,)), sem((n_col,)), sem((n_col,)), sem((n_col,)),
        sem((half,)), sem((depth,)), sem((depth,)), sem((1,)), sem((half,)), sem((half,)), sem((half,)),
    ]
    return pl.pallas_call(
        functools.partial(kernel, n_row, n_col, factor),
        out_shape=(
            jax.ShapeDtypeStruct((tile, hidden), BF),
            jax.ShapeDtypeStruct((tile, width), BF),
            jax.ShapeDtypeStruct((width, hidden), F32),
            jax.ShapeDtypeStruct((width, hidden), F32),
            jax.ShapeDtypeStruct((hidden,), F32),
        ),
        in_specs=[any_, any_, smem, smem, any_, any_, vmem, any_],
        out_specs=(vmem,) * 5,
        scratch_shapes=scratch,
        compiler_params=pltpu.CompilerParams(
            collective_id=0, has_side_effects=True, vmem_limit_bytes=48 * 1024 * 1024
        ),
    )(features, adjacency, tile_pos, tile_count, w_self, w_neigh, bias, upstream)


def solution(mesh):
    placed = (
        P(("row", "col"), None),
        P("row", "col", None, None, None),
        P("row", "col", None),
        P("row", "col"),
        P(),
        P(),
        P(),
        P(("row", "col"), None),
    )
    return jax.shard_map(
        body,
        mesh=mesh,
        in_specs=placed,
        out_specs=(P(("row", "col"), None), P(("row", "col"), None), P(), P(), P()),
        check_vma=False,
    )
```

```python
import functools
import math

import jax
import jax.numpy as jnp
from jax import lax
from jax.experimental import pallas as pl
from jax.experimental.pallas import tpu as pltpu
from jax.sharding import PartitionSpec as P

BF = jnp.bfloat16
F32 = jnp.float32
MESH = pl.DeviceIdType.MESH


def dot(a, b):
    return jnp.dot(a, b, preferred_element_type=F32)


def dot_nt(a, b):
    return lax.dot_general(a, b, (((1,), (1,)), ((), ())), preferred_element_type=F32)


def kernel(
    n_row, n_col, factor,
    feat, adj, pos_h, cnt_h, wself, wneigh, bias_h, up,
    hid_o, gf_o, gs_o, gn_o, gb_o,
    pos, cnt, bias, adj_v, dense, gath, f2, up2, w_v, deg, base, inv_row, inv_col, part, agg_v, gpre, pre,
    c_send, c_recv, own, x_send, x_recv, z_send, z_recv,
    g_units, g1_send, g1_recv, g2_send, g2_recv, gfull,
    loc_sem, send_sem, gath_sem, f2_sem, up_sem, deg_sem, part_sem,
    c_sem, x_sem, z_sem, g1_sem, g2_sem, g3_sem, g4_sem,
):
    row = lax.axis_index("row")
    col = lax.axis_index("col")
    depth = n_row // 4
    half = n_row // 2
    core = row % 2
    x = (row // 2) % 2
    z = row // 4
    tile = feat.shape[0]
    slots = adj.shape[2]
    width = feat.shape[1]
    rows = n_col * tile
    units = g_units.shape[0]
    per = units // n_row

    def row_of(dz, dx, dc):
        return (((z + dz) % depth) * 2 + (x + dx) % 2) * 2 + (core + dc) % 2

    def chip(j):
        return row_of(j % depth, j // depth, 0)

    sends = []

    def send(src, dst, sem, to_row, to_col=None):
        copy = pltpu.make_async_remote_copy(
            src_ref=src, dst_ref=dst, send_sem=send_sem.at[len(sends)], recv_sem=sem,
            device_id=(to_row, col if to_col is None else to_col), device_id_type=MESH,
        )
        copy.start()
        sends.append(copy)

    def got(dst, sem):
        pltpu.make_async_remote_copy(
            src_ref=dst, dst_ref=dst, send_sem=send_sem.at[0], recv_sem=sem,
            device_id=(row_of(0, 0, 1), col), device_id_type=MESH,
        ).wait_recv()

    core_peer = row_of(0, 0, 1)
    x_peer = row_of(0, 1, 0)

    barrier = pltpu.get_barrier_semaphore()
    for j in range(1, half):
        pl.semaphore_signal(barrier, inc=1, device_id=(chip(j), col), device_id_type=MESH)
    pl.semaphore_signal(barrier, inc=1, device_id=(core_peer, col), device_id_type=MESH)
    for k in range(1, n_col):
        pl.semaphore_signal(barrier, inc=1, device_id=(row, (col + k) % n_col), device_id_type=MESH)

    own_rows = pl.ds(pl.multiple_of(col * tile, tile), tile)
    locals_ = [
        pltpu.make_async_copy(adj.at[0, 0], adj_v, loc_sem.at[0]),
        pltpu.make_async_copy(feat, gath.at[pl.ds(0, tile)], loc_sem.at[1]),
        pltpu.make_async_copy(feat, f2.at[own_rows], loc_sem.at[2]),
        pltpu.make_async_copy(up, up2.at[own_rows], loc_sem.at[3]),
        pltpu.make_async_copy(wself, w_v.at[0], loc_sem.at[4]),
        pltpu.make_async_copy(wneigh, w_v.at[1], loc_sem.at[5]),
        pltpu.make_async_copy(bias_h, bias, loc_sem.at[6]),
        pltpu.make_async_copy(pos_h, pos, loc_sem.at[7]),
        pltpu.make_async_copy(cnt_h, cnt, loc_sem.at[8]),
    ]
    for copy in locals_:
        copy.start()
    pl.semaphore_wait(barrier, half - 1 + 1 + n_col - 1)

    def slot(q):
        return gath.at[pl.ds(q * tile, tile)]

    for k in range(1, depth):
        q = depth - k
        send(feat, slot(q), gath_sem.at[q], row_of(k, 0, 0))
    send(feat, slot(depth), gath_sem.at[depth], x_peer)
    send(feat, slot(half), gath_sem.at[half], core_peer)
    for k in range(1, n_col):
        send(feat, f2.at[own_rows], f2_sem.at[n_col - k], row, (col + k) % n_col)
        send(up, up2.at[own_rows], up_sem.at[n_col - k], row, (col + k) % n_col)

    locals_[7].wait()
    locals_[8].wait()
    filled = cnt[0, 0]
    places = [jnp.where(t < filled, pos[0, 0, t], -1) for t in range(slots)]
    locals_[0].wait()

    def place(i, carry):
        r = i // n_row
        q = i % n_row
        target = r * n_row + row_of(q % depth, (q % half) // depth, q // half)
        found = jnp.int32(-1)
        for t in range(slots):
            found = jnp.where(places[t] == target, t, found)
        block = adj_v[jnp.maximum(found, 0)]
        keep = jnp.full((tile, tile), found, jnp.int32) >= 0
        block = jnp.where(keep, block.astype(F32), 0.0).astype(BF)
        dense[pl.ds(pl.multiple_of(r * tile, tile), tile), pl.ds(pl.multiple_of(q * tile, tile), tile)] = block
        return carry

    lax.fori_loop(0, n_col * n_row, place, 0)

    for k in range(1, depth):
        q = depth - k
        got(slot(q), gath_sem.at[q])
        send(slot(q), slot(depth + q), gath_sem.at[depth + q], x_peer)
        send(slot(q), slot(half + q), gath_sem.at[half + q], core_peer)

    ones = jnp.ones((16, dense.shape[1]), BF)
    deg[col] = dot_nt(ones, dense[...])[0:8]
    for k in range(1, n_col):
        send(deg.at[col], deg.at[col], deg_sem.at[n_col - k], row, (col + k) % n_col)

    for q in [depth] + [2 * depth - k for k in range(1, depth)]:
        got(slot(q), gath_sem.at[q])
        send(slot(q), slot(half + q), gath_sem.at[half + q], core_peer)

    locals_[1].wait()
    partial_value = dot(dense[:, : half * tile], gath[: half * tile])

    for copy in locals_[2:7]:
        copy.wait()
    for k in range(1, n_col):
        sender = (col + k) % n_col
        sender_rows = pl.ds(pl.multiple_of(sender * tile, tile), tile)
        got(f2.at[sender_rows], f2_sem.at[k])
        got(up2.at[sender_rows], up_sem.at[k])
        got(deg.at[sender], deg_sem.at[k])
    base[...] = dot(f2[...], w_v[0]) + bias[...].reshape(1, -1)
    total = deg[0]
    for k in range(1, n_col):
        total = total + deg[k]
    inv_row[...] = 1.0 / jnp.sqrt(1.0 + total)
    for r in range(n_col):
        line = inv_row[0:1, r * tile : (r + 1) * tile]
        inv_col[r * tile : (r + 1) * tile] = jnp.broadcast_to(line, (tile, tile)).T

    for q in range(half, n_row):
        got(slot(q), gath_sem.at[q])
    partial_value += dot(dense[:, half * tile :], gath[half * tile :])
    part[col] = partial_value.astype(BF)
    for k in range(1, n_col):
        send(part.at[col], part.at[col], part_sem.at[n_col - k], row, (col + k) % n_col)
    for k in range(1, n_col):
        got(part.at[(col + k) % n_col], part_sem.at[k])

    summed = part[0].astype(F32)
    for k in range(1, n_col):
        summed = summed + part[k].astype(F32)
    agg_v[...] = (summed * inv_col[...]).astype(BF)
    pre[...] = base[...] + dot(agg_v[...], w_v[1])
    preact = pre[...]
    gate = jax.nn.sigmoid(preact)
    gpre[...] = (up2[...].astype(F32) * (gate + preact * gate * (1.0 - gate))).astype(BF)
    grad_agg = (dot_nt(w_v[1], gpre[...]) * inv_row[0:1]).astype(BF)

    order = list(range(depth, half)) + list(range(depth))
    for j in order[::2]:
        both = dot(grad_agg, dense[:, (half + j) * tile : (half + j + 2) * tile]).astype(BF)
        for i in (0, 1):
            c_send[j + i] = both[:, i * tile : (i + 1) * tile]
            send(c_send.at[j + i], c_recv.at[j + i], c_sem.at[j + i], core_peer)

    gp = gpre[...]
    upper = dot(f2[...].T, gp)
    lower = dot(agg_v[...].T, gp)
    lanes = gp.shape[1] // 128
    for u in range(units):
        r0, l0 = (u // lanes) * 16, (u % lanes) * 128
        src = upper if r0 < width else lower
        g_units[u] = src[r0 % width : r0 % width + 16, l0 : l0 + 128]
    colsum = dot(jnp.ones((8, gp.shape[0]), BF), gp)
    bias_unit = jnp.concatenate([colsum[:, i * 128 : (i + 1) * 128] for i in range(lanes)], axis=0).astype(BF)
    for j in range(half):
        target = row_of(j % depth, j // depth, 1)
        g1_send[j * per : (j + 1) * per] = g_units[pl.ds(target * per, per)].astype(BF)
    g1_send[half * per] = bias_unit
    send(g1_send, g1_recv, g1_sem.at[0], core_peer)

    for j in order[::2]:
        both = dot(grad_agg, dense[:, j * tile : (j + 2) * tile])
        for i in (0, 1):
            own[j + i] = both[:, i * tile : (i + 1) * tile]

    for dz in list(range(1, depth)) + [0]:
        j = depth + dz
        got(c_recv.at[j], c_sem.at[j])
        x_send[dz] = (own[j] + c_recv[j].astype(F32)).astype(BF)
        send(x_send.at[dz], x_recv.at[dz], x_sem.at[dz], x_peer)

    got(g1_recv, g1_sem.at[0])
    for j in list(range(1, half)) + [0]:
        target = chip(j)
        g2_send[j, 0:per] = (
            g_units[pl.ds(target * per, per)] + g1_recv[j * per : (j + 1) * per].astype(F32)
        ).astype(BF)
        g2_send[j, per] = (bias_unit.astype(F32) + g1_recv[half * per].astype(F32)).astype(BF)
        if j:
            back = (j // depth) * depth + (depth - j % depth) % depth
            send(g2_send.at[j], g2_recv.at[back], g2_sem.at[back], target)
        else:
            g2_recv[0] = g2_send[0]

    for dz in list(range(1, depth)) + [0]:
        got(c_recv.at[dz], c_sem.at[dz])
        got(x_recv.at[dz], x_sem.at[dz])
        value = own[dz] + c_recv[dz].astype(F32) + x_recv[dz].astype(F32)
        if dz:
            z_send[dz - 1] = value.astype(BF)
            send(z_send.at[dz - 1], z_recv.at[dz - 1], z_sem.at[dz - 1], row_of(dz, 0, 0))
        else:
            own[0] = value

    for j in range(1, half):
        got(g2_recv.at[j], g2_sem.at[j])
    piece = jnp.zeros(g2_recv.shape[1:], F32)
    for a in range(half):
        rel = ((a % 2 + 2 - x) % 2) * depth + (a // 2 + depth - z) % depth
        piece = piece + g2_recv[rel].astype(F32)
    piece = piece * factor
    gfull[row] = piece[0:per].astype(BF)
    for j in range(1, half):
        back = (j // depth) * depth + (depth - j % depth) % depth
        send(gfull.at[row], gfull.at[row], g3_sem.at[back], chip(j))
    send(gfull.at[row], gfull.at[row], g4_sem.at[0], core_peer)
    sums = piece[per]
    gb_o[...] = jnp.concatenate([sums[i * 8 : i * 8 + 1] for i in range(lanes)], axis=1).reshape(-1)

    preact = pre[own_rows]
    hid_o[...] = (preact * jax.nn.sigmoid(preact)).astype(BF)
    value = own[0]
    for dz in range(1, depth):
        got(z_recv.at[dz - 1], z_sem.at[dz - 1])
        value = value + z_recv[dz - 1].astype(F32)
    gf_o[...] = (dot_nt(gpre[own_rows], w_v[0]) + value.T).astype(BF)

    for j in range(1, half):
        d = chip(j)
        got(gfull.at[d], g3_sem.at[j])
        send(gfull.at[d], gfull.at[d], g4_sem.at[j], core_peer)
    for j in range(half):
        got(gfull.at[row_of(j % depth, j // depth, 1)], g4_sem.at[j])
    for u in range(units):
        r0, l0 = (u // lanes) * 16, (u % lanes) * 128
        out = gs_o if r0 < width else gn_o
        r0 = r0 % width
        out[r0 : r0 + 16, l0 : l0 + 128] = gfull[u // per, u % per].astype(F32)

    for copy in sends:
        copy.wait_send()


def write_out(*refs):
    sems = refs[10]
    copies = [pltpu.make_async_copy(refs[i], refs[5 + i], sems.at[i]) for i in range(5)]
    for copy in copies:
        copy.start()
    for copy in copies:
        copy.wait()


def body(features, adjacency, tile_pos, tile_count, w_self, w_neigh, bias, upstream):
    n_row = lax.axis_size("row")
    n_col = lax.axis_size("col")
    tile, width = features.shape
    hidden = upstream.shape[1]
    slots = adjacency.shape[2]
    rows = n_col * tile
    depth, half = n_row // 4, n_row // 2
    units = (2 * width // 16) * (hidden // 128)
    per = units // n_row
    factor = 1.0 / math.sqrt(tile * n_row * n_col)
    sem = pltpu.SemaphoreType.DMA
    n_sends = (
        (depth - 1) + 2 + 2 * (n_col - 1) + 2 * (depth - 1) + (n_col - 1) + depth + (n_col - 1)
        + half + 1 + depth + (half - 1) + (depth - 1) + (half - 1) + half
    )
    hbm = pl.BlockSpec(memory_space=pltpu.HBM)
    vmem = pl.BlockSpec(memory_space=pltpu.VMEM)
    scratch = [
        pltpu.SMEM(tile_pos.shape, jnp.int32),
        pltpu.SMEM(tile_count.shape, jnp.int32),
        pltpu.VMEM(bias.shape, F32),
        pltpu.VMEM((slots, tile, tile), BF),
        pltpu.VMEM((rows, n_row * tile), BF),
        pltpu.VMEM((n_row * tile, width), BF),
        pltpu.VMEM((rows, width), BF),
        pltpu.VMEM((rows, hidden), BF),
        pltpu.VMEM((2, width, hidden), BF),
        pltpu.VMEM((n_col, 8, rows), F32),
        pltpu.VMEM((rows, hidden), F32),
        pltpu.VMEM((8, rows), F32),
        pltpu.VMEM((rows, width), F32),
        pltpu.VMEM((n_col, rows, width), BF),
        pltpu.VMEM((rows, width), BF),
        pltpu.VMEM((rows, hidden), BF),
        pltpu.VMEM((rows, hidden), F32),
        pltpu.VMEM((half, width, tile), BF),
        pltpu.VMEM((half, width, tile), BF),
        pltpu.VMEM((half, width, tile), F32),
        pltpu.VMEM((depth, width, tile), BF),
        pltpu.VMEM((depth, width, tile), BF),
        pltpu.VMEM((depth - 1, width, tile), BF),
        pltpu.VMEM((depth - 1, width, tile), BF),
        pltpu.VMEM((units, 16, 128), F32),
        pltpu.VMEM((half * per + 1, 16, 128), BF),
        pltpu.VMEM((half * per + 1, 16, 128), BF),
        pltpu.VMEM((half, per + 1, 16, 128), BF),
        pltpu.VMEM((half, per + 1, 16, 128), BF),
        pltpu.VMEM((n_row, per, 16, 128), BF),
        sem((9,)), sem((n_sends,)), sem((n_row,)), sem((n_col,)), sem((n_col,)), sem((n_col,)), sem((n_col,)),
        sem((half,)), sem((depth,)), sem((depth,)), sem((1,)), sem((half,)), sem((half,)), sem((half,)),
    ]
    shapes = (
        jax.ShapeDtypeStruct((tile, hidden), BF),
        jax.ShapeDtypeStruct((tile, width), BF),
        jax.ShapeDtypeStruct((width, hidden), F32),
        jax.ShapeDtypeStruct((width, hidden), F32),
        jax.ShapeDtypeStruct((hidden,), F32),
    )
    results = pl.pallas_call(
        functools.partial(kernel, n_row, n_col, factor),
        out_shape=shapes,
        in_specs=[hbm] * 8,
        out_specs=(vmem,) * 5,
        scratch_shapes=scratch,
        compiler_params=pltpu.CompilerParams(
            collective_id=0, has_side_effects=True, vmem_limit_bytes=62 * 1024 * 1024
        ),
    )(features, adjacency, tile_pos, tile_count, w_self, w_neigh, bias, upstream)
    return pl.pallas_call(
        write_out,
        out_shape=shapes,
        in_specs=[vmem] * 5,
        out_specs=(hbm,) * 5,
        scratch_shapes=[sem((5,))],
    )(*results)


def solution(mesh):
    placed = (
        P(("row", "col"), None),
        P("row", "col", None, None, None),
        P("row", "col", None),
        P("row", "col"),
        P(),
        P(),
        P(),
        P(("row", "col"), None),
    )
    return jax.shard_map(
        body,
        mesh=mesh,
        in_specs=placed,
        out_specs=(P(("row", "col"), None), P(("row", "col"), None), P(), P(), P()),
        check_vma=False,
    )
```

```python
import functools
import math

import jax
import jax.numpy as jnp
from jax import lax
from jax.experimental import pallas as pl
from jax.experimental.pallas import tpu as pltpu
from jax.sharding import PartitionSpec as P

BF = jnp.bfloat16
F32 = jnp.float32
MESH = pl.DeviceIdType.MESH


def dot(a, b):
    return jnp.dot(a, b, preferred_element_type=F32)


def dot_nt(a, b):
    return lax.dot_general(a, b, (((1,), (1,)), ((), ())), preferred_element_type=F32)


def kernel(
    n_row, n_col, factor,
    feat, adj, pos_h, cnt_h, wself, wneigh, bias_h, up,
    hid_o, gf_o, gs_o, gn_o, gb_o,
    pos, cnt, bias, adj_v, dense, gath, f2, up2, w_v, deg, base, inv_row, inv_col, part, agg_v, gpre, pre,
    c_send, c_recv, own, x_send, x_recv, z_send, z_recv,
    g_units, g1_send, g1_recv, g2_send, g2_recv, gfull,
    loc_sem, send_sem, gath_sem, f2_sem, up_sem, deg_sem, part_sem,
    c_sem, x_sem, z_sem, g1_sem, g2_sem, g3_sem, g4_sem,
):
    row = lax.axis_index("row")
    col = lax.axis_index("col")
    depth = n_row // 4
    half = n_row // 2
    core = row % 2
    x = (row // 2) % 2
    z = row // 4
    tile = feat.shape[0]
    slots = adj.shape[2]
    width = feat.shape[1]
    rows = n_col * tile
    units = g_units.shape[0]
    per = units // n_row

    def row_of(dz, dx, dc):
        return (((z + dz) % depth) * 2 + (x + dx) % 2) * 2 + (core + dc) % 2

    def chip(j):
        return row_of(j % depth, j // depth, 0)

    sends = []

    def send(src, dst, sem, to_row, to_col=None):
        copy = pltpu.make_async_remote_copy(
            src_ref=src, dst_ref=dst, send_sem=send_sem.at[len(sends)], recv_sem=sem,
            device_id=(to_row, col if to_col is None else to_col), device_id_type=MESH,
        )
        copy.start()
        sends.append(copy)

    def got(dst, sem):
        pltpu.make_async_remote_copy(
            src_ref=dst, dst_ref=dst, send_sem=send_sem.at[0], recv_sem=sem,
            device_id=(row_of(0, 0, 1), col), device_id_type=MESH,
        ).wait_recv()

    core_peer = row_of(0, 0, 1)
    x_peer = row_of(0, 1, 0)

    barrier = pltpu.get_barrier_semaphore()
    for j in range(1, half):
        pl.semaphore_signal(barrier, inc=1, device_id=(chip(j), col), device_id_type=MESH)
    pl.semaphore_signal(barrier, inc=1, device_id=(core_peer, col), device_id_type=MESH)
    for k in range(1, n_col):
        pl.semaphore_signal(barrier, inc=1, device_id=(row, (col + k) % n_col), device_id_type=MESH)

    own_rows = pl.ds(pl.multiple_of(col * tile, tile), tile)
    locals_ = [
        pltpu.make_async_copy(adj.at[0, 0], adj_v, loc_sem.at[0]),
        pltpu.make_async_copy(feat, gath.at[pl.ds(0, tile)], loc_sem.at[1]),
        pltpu.make_async_copy(feat, f2.at[own_rows], loc_sem.at[2]),
        pltpu.make_async_copy(up, up2.at[own_rows], loc_sem.at[3]),
        pltpu.make_async_copy(wself, w_v.at[0], loc_sem.at[4]),
        pltpu.make_async_copy(wneigh, w_v.at[1], loc_sem.at[5]),
        pltpu.make_async_copy(bias_h, bias, loc_sem.at[6]),
        pltpu.make_async_copy(pos_h, pos, loc_sem.at[7]),
        pltpu.make_async_copy(cnt_h, cnt, loc_sem.at[8]),
    ]
    for copy in locals_:
        copy.start()
    pl.semaphore_wait(barrier, half - 1 + 1 + n_col - 1)

    def slot(q):
        return gath.at[pl.ds(q * tile, tile)]

    for k in range(1, depth):
        q = depth - k
        send(feat, slot(q), gath_sem.at[q], row_of(k, 0, 0))
    send(feat, slot(depth), gath_sem.at[depth], x_peer)
    send(feat, slot(half), gath_sem.at[half], core_peer)
    for k in range(1, n_col):
        send(feat, f2.at[own_rows], f2_sem.at[n_col - k], row, (col + k) % n_col)
        send(up, up2.at[own_rows], up_sem.at[n_col - k], row, (col + k) % n_col)

    locals_[7].wait()
    locals_[8].wait()
    filled = cnt[0, 0, 0]
    places = [jnp.where(t < filled, pos[0, 0, t], -1) for t in range(slots)]
    locals_[0].wait()

    def place(i, carry):
        r = i // n_row
        q = i % n_row
        target = r * n_row + row_of(q % depth, (q % half) // depth, q // half)
        found = jnp.int32(-1)
        for t in range(slots):
            found = jnp.where(places[t] == target, t, found)
        block = adj_v[jnp.maximum(found, 0)]
        keep = jnp.full((tile, tile), found, jnp.int32) >= 0
        block = jnp.where(keep, block.astype(F32), 0.0).astype(BF)
        dense[pl.ds(pl.multiple_of(r * tile, tile), tile), pl.ds(pl.multiple_of(q * tile, tile), tile)] = block
        return carry

    lax.fori_loop(0, n_col * n_row, place, 0)

    for k in range(1, depth):
        q = depth - k
        got(slot(q), gath_sem.at[q])
        send(slot(q), slot(depth + q), gath_sem.at[depth + q], x_peer)
        send(slot(q), slot(half + q), gath_sem.at[half + q], core_peer)

    deg[col] = dot(dense[...], jnp.ones((dense.shape[1], tile), BF)).T[0:8]
    for k in range(1, n_col):
        send(deg.at[col], deg.at[col], deg_sem.at[n_col - k], row, (col + k) % n_col)

    for q in [depth] + [2 * depth - k for k in range(1, depth)]:
        got(slot(q), gath_sem.at[q])
        send(slot(q), slot(half + q), gath_sem.at[half + q], core_peer)

    locals_[1].wait()
    partial_value = dot(dense[:, : half * tile], gath[: half * tile])

    for q in range(half, n_row):
        got(slot(q), gath_sem.at[q])
    partial_value += dot(dense[:, half * tile :], gath[half * tile :])
    part[col] = partial_value.astype(BF)
    for k in range(1, n_col):
        send(part.at[col], part.at[col], part_sem.at[n_col - k], row, (col + k) % n_col)
    for copy in locals_[2:7]:
        copy.wait()
    for k in range(1, n_col):
        sender = (col + k) % n_col
        sender_rows = pl.ds(pl.multiple_of(sender * tile, tile), tile)
        got(f2.at[sender_rows], f2_sem.at[k])
        got(up2.at[sender_rows], up_sem.at[k])
        got(deg.at[sender], deg_sem.at[k])
    base[...] = dot(f2[...], w_v[0]) + bias[...].reshape(1, -1)
    total = deg[0]
    for k in range(1, n_col):
        total = total + deg[k]
    inv_row[...] = 1.0 / jnp.sqrt(1.0 + total)
    for r in range(n_col):
        line = inv_row[0:1, r * tile : (r + 1) * tile]
        inv_col[r * tile : (r + 1) * tile] = jnp.broadcast_to(line, (tile, tile)).T

    for k in range(1, n_col):
        got(part.at[(col + k) % n_col], part_sem.at[k])

    summed = part[0].astype(F32)
    for k in range(1, n_col):
        summed = summed + part[k].astype(F32)
    agg_v[...] = (summed * inv_col[...]).astype(BF)
    pre[...] = base[...] + dot(agg_v[...], w_v[1])
    preact = pre[...]
    gate = jax.nn.sigmoid(preact)
    gpre[...] = (up2[...].astype(F32) * (gate + preact * gate * (1.0 - gate))).astype(BF)
    grad_agg = (dot_nt(w_v[1], gpre[...]) * inv_row[0:1]).astype(BF)

    gp = gpre[...]
    upper = dot(f2[...].T, gp)
    lower = dot(agg_v[...].T, gp)
    lanes = gp.shape[1] // 128
    for u in range(units):
        r0, l0 = (u // lanes) * 16, (u % lanes) * 128
        src = upper if r0 < width else lower
        g_units[u] = src[r0 % width : r0 % width + 16, l0 : l0 + 128]
    colsum = dot(jnp.ones((8, gp.shape[0]), BF), gp)
    bias_unit = jnp.concatenate([colsum[:, i * 128 : (i + 1) * 128] for i in range(lanes)], axis=0).astype(BF)
    for j in range(half):
        target = row_of(j % depth, j // depth, 1)
        g1_send[j * per : (j + 1) * per] = g_units[pl.ds(target * per, per)].astype(BF)
    g1_send[half * per] = bias_unit
    send(g1_send, g1_recv, g1_sem.at[0], core_peer)

    order = list(range(depth, half)) + list(range(depth))
    for j in order[::2]:
        both = dot(grad_agg, dense[:, (half + j) * tile : (half + j + 2) * tile]).astype(BF)
        for i in (0, 1):
            c_send[j + i] = both[:, i * tile : (i + 1) * tile]
            send(c_send.at[j + i], c_recv.at[j + i], c_sem.at[j + i], core_peer)

    for j in order[::2]:
        both = dot(grad_agg, dense[:, j * tile : (j + 2) * tile])
        for i in (0, 1):
            own[j + i] = both[:, i * tile : (i + 1) * tile]

    got(g1_recv, g1_sem.at[0])
    for j in list(range(1, half)) + [0]:
        target = chip(j)
        g2_send[j, 0:per] = (
            g_units[pl.ds(target * per, per)] + g1_recv[j * per : (j + 1) * per].astype(F32)
        ).astype(BF)
        g2_send[j, per] = (bias_unit.astype(F32) + g1_recv[half * per].astype(F32)).astype(BF)
        if j:
            back = (j // depth) * depth + (depth - j % depth) % depth
            send(g2_send.at[j], g2_recv.at[back], g2_sem.at[back], target)
        else:
            g2_recv[0] = g2_send[0]

    for dz in list(range(1, depth)) + [0]:
        j = depth + dz
        got(c_recv.at[j], c_sem.at[j])
        x_send[dz] = (own[j] + c_recv[j].astype(F32)).astype(BF)
        send(x_send.at[dz], x_recv.at[dz], x_sem.at[dz], x_peer)

    for dz in list(range(1, depth)) + [0]:
        got(c_recv.at[dz], c_sem.at[dz])
        got(x_recv.at[dz], x_sem.at[dz])
        value = own[dz] + c_recv[dz].astype(F32) + x_recv[dz].astype(F32)
        if dz:
            z_send[dz - 1] = value.astype(BF)
            send(z_send.at[dz - 1], z_recv.at[dz - 1], z_sem.at[dz - 1], row_of(dz, 0, 0))
        else:
            own[0] = value

    for j in range(1, half):
        got(g2_recv.at[j], g2_sem.at[j])
    piece = jnp.zeros(g2_recv.shape[1:], F32)
    for a in range(half):
        rel = ((a % 2 + 2 - x) % 2) * depth + (a // 2 + depth - z) % depth
        piece = piece + g2_recv[rel].astype(F32)
    piece = piece * factor
    gfull[row] = piece[0:per].astype(BF)
    for j in range(1, half):
        back = (j // depth) * depth + (depth - j % depth) % depth
        send(gfull.at[row], gfull.at[row], g3_sem.at[back], chip(j))
    send(gfull.at[row], gfull.at[row], g4_sem.at[0], core_peer)
    sums = piece[per]
    gb_o[...] = jnp.concatenate([sums[i * 8 : i * 8 + 1] for i in range(lanes)], axis=1).reshape(-1)

    preact = pre[own_rows]
    hid_o[...] = (preact * jax.nn.sigmoid(preact)).astype(BF)
    value = own[0]
    for dz in range(1, depth):
        got(z_recv.at[dz - 1], z_sem.at[dz - 1])
        value = value + z_recv[dz - 1].astype(F32)
    gf_o[...] = (dot_nt(gpre[own_rows], w_v[0]) + value.T).astype(BF)

    for j in range(1, half):
        d = chip(j)
        got(gfull.at[d], g3_sem.at[j])
        send(gfull.at[d], gfull.at[d], g4_sem.at[j], core_peer)
    for j in range(half):
        got(gfull.at[row_of(j % depth, j // depth, 1)], g4_sem.at[j])
    for u in range(units):
        r0, l0 = (u // lanes) * 16, (u % lanes) * 128
        out = gs_o if r0 < width else gn_o
        r0 = r0 % width
        out[r0 : r0 + 16, l0 : l0 + 128] = gfull[u // per, u % per].astype(F32)

    for copy in sends:
        copy.wait_send()


def write_out(*refs):
    sems = refs[10]
    copies = [pltpu.make_async_copy(refs[i], refs[5 + i], sems.at[i]) for i in range(5)]
    for copy in copies:
        copy.start()
    for copy in copies:
        copy.wait()


def body(features, adjacency, tile_pos, tile_count, w_self, w_neigh, bias, upstream):
    n_row = lax.axis_size("row")
    n_col = lax.axis_size("col")
    tile, width = features.shape
    hidden = upstream.shape[1]
    slots = adjacency.shape[2]
    rows = n_col * tile
    depth, half = n_row // 4, n_row // 2
    units = (2 * width // 16) * (hidden // 128)
    per = units // n_row
    factor = 1.0 / math.sqrt(tile * n_row * n_col)
    sem = pltpu.SemaphoreType.DMA
    n_sends = (
        (depth - 1) + 2 + 2 * (n_col - 1) + 2 * (depth - 1) + (n_col - 1) + depth + (n_col - 1)
        + half + 1 + depth + (half - 1) + (depth - 1) + (half - 1) + half
    )
    hbm = pl.BlockSpec(memory_space=pltpu.HBM)
    vmem = pl.BlockSpec(memory_space=pltpu.VMEM)
    scratch = [
        pltpu.SMEM(tile_pos.shape, jnp.int32),
        pltpu.SMEM((1, 1, 1), jnp.int32),
        pltpu.VMEM(bias.shape, F32),
        pltpu.VMEM((slots, tile, tile), BF),
        pltpu.VMEM((rows, n_row * tile), BF),
        pltpu.VMEM((n_row * tile, width), BF),
        pltpu.VMEM((rows, width), BF),
        pltpu.VMEM((rows, hidden), BF),
        pltpu.VMEM((2, width, hidden), BF),
        pltpu.VMEM((n_col, 8, rows), F32),
        pltpu.VMEM((rows, hidden), F32),
        pltpu.VMEM((8, rows), F32),
        pltpu.VMEM((rows, width), F32),
        pltpu.VMEM((n_col, rows, width), BF),
        pltpu.VMEM((rows, width), BF),
        pltpu.VMEM((rows, hidden), BF),
        pltpu.VMEM((rows, hidden), F32),
        pltpu.VMEM((half, width, tile), BF),
        pltpu.VMEM((half, width, tile), BF),
        pltpu.VMEM((half, width, tile), F32),
        pltpu.VMEM((depth, width, tile), BF),
        pltpu.VMEM((depth, width, tile), BF),
        pltpu.VMEM((depth - 1, width, tile), BF),
        pltpu.VMEM((depth - 1, width, tile), BF),
        pltpu.VMEM((units, 16, 128), F32),
        pltpu.VMEM((half * per + 1, 16, 128), BF),
        pltpu.VMEM((half * per + 1, 16, 128), BF),
        pltpu.VMEM((half, per + 1, 16, 128), BF),
        pltpu.VMEM((half, per + 1, 16, 128), BF),
        pltpu.VMEM((n_row, per, 16, 128), BF),
        sem((9,)), sem((n_sends,)), sem((n_row,)), sem((n_col,)), sem((n_col,)), sem((n_col,)), sem((n_col,)),
        sem((half,)), sem((depth,)), sem((depth,)), sem((1,)), sem((half,)), sem((half,)), sem((half,)),
    ]
    shapes = (
        jax.ShapeDtypeStruct((tile, hidden), BF),
        jax.ShapeDtypeStruct((tile, width), BF),
        jax.ShapeDtypeStruct((width, hidden), F32),
        jax.ShapeDtypeStruct((width, hidden), F32),
        jax.ShapeDtypeStruct((hidden,), F32),
    )
    results = pl.pallas_call(
        functools.partial(kernel, n_row, n_col, factor),
        out_shape=shapes,
        in_specs=[hbm] * 8,
        out_specs=(vmem,) * 5,
        scratch_shapes=scratch,
        compiler_params=pltpu.CompilerParams(
            collective_id=0, has_side_effects=True, vmem_limit_bytes=62 * 1024 * 1024
        ),
    )(features, adjacency, tile_pos, tile_count.reshape(1, 1, 1), w_self, w_neigh, bias, upstream)
    return pl.pallas_call(
        write_out,
        out_shape=shapes,
        in_specs=[vmem] * 5,
        out_specs=(hbm,) * 5,
        scratch_shapes=[sem((5,))],
    )(*results)


def solution(mesh):
    placed = (
        P(("row", "col"), None),
        P("row", "col", None, None, None),
        P("row", "col", None),
        P("row", "col"),
        P(),
        P(),
        P(),
        P(("row", "col"), None),
    )
    return jax.shard_map(
        body,
        mesh=mesh,
        in_specs=placed,
        out_specs=(P(("row", "col"), None), P(("row", "col"), None), P(), P(), P()),
        check_vma=False,
    )
```
